256 devices in a mesh: seq: 64 (over x, y, z_hi, core), ch: 4 (over z_lo).
Axes of the slice: x: 4, y: 4, z: 8 (z_hi: 2, z_lo: 4; z = z_hi * 4 + z_lo), core: 2. Of those that a mesh axis runs over, the one named last changes fastest.
Arguments:
- values: bfloat16 [16384, 2048], P('seq', 'ch'), may hold values from -7.5 to 7.5
- gates: bfloat16 [16384, 2048], P('seq', 'ch'), may hold values from -6 to 6
- filters: float32 [16384, 2048], P('seq', 'ch'), may hold values from -1.1 to 1.1
- skip: float32 [2048], P('ch'), may hold values from -4 to 4
- cotangent: bfloat16 [16384, 2048], P('seq', 'ch'), may hold values from -6 to 6
- flagged: int32 [16384], P('seq'), may hold values 0 or 1
Outputs:
- mixed: bfloat16 [16384, 2048], P('seq', 'ch')
- value_grad: bfloat16 [16384, 2048], P('seq', 'ch')
- gate_grad: bfloat16 [16384, 2048], P('seq', 'ch')
- filter_grad: float32 [16384, 2048], P('seq', 'ch')
- skip_grad: float32 [2048], P('ch')
The draws below stay inside these ranges and needn't reach their ends.
All inputs are finite; a program needn't handle non-finite values. No bound on the sum of `flagged` on one device may be relied on, other than what follows from the above.
Results may differ from the reference program's by a relative error of at most 0.001.
Values sent between devices are 32-bit elements; how exact they have to be, the bound alone decides.
A program may use at most 128 MiB of HBM per device.

```python
import jax
import jax.numpy as jnp

D = 2048
NUCLEOTIDE_COUNT = 16384


def draw_filters(key, part):
    key = jax.random.fold_in(key, 7)
    derived_seeds = jax.random.split(key, 8)
    nucleotide_offset = jnp.arange(NUCLEOTIDE_COUNT, dtype=jnp.float32)[:, None]
    slow_share = 0.5
    stochastic_jitter = jax.random.truncated_normal(derived_seeds[4], -4.0, 4.0, (NUCLEOTIDE_COUNT, D), jnp.float32)
    slow_mask = jax.random.uniform(derived_seeds[0], (D,), jnp.float32) < slow_share
    slow_rate = jnp.exp(jax.random.uniform(derived_seeds[1], (D,), jnp.float32, jnp.log(0.1), jnp.log(1.5))) / NUCLEOTIDE_COUNT
    fast_rate = jax.random.uniform(derived_seeds[2], (D,), jnp.float32, 1.0 / 50.0, 1.0 / 30.0)
    decay_speed = jnp.where(slow_mask, slow_rate, fast_rate)
    clustered_marker = jax.random.randint(derived_seeds[3], (3,), 0, NUCLEOTIDE_COUNT).astype(jnp.float32)
    clustered_erasure = jnp.prod(jnp.where(nucleotide_offset[:, :, None] >= clustered_marker[None, None, :], 0.75, 1.0), axis=2)
    tail_size = jnp.exp(jax.random.uniform(derived_seeds[5], (D,), jnp.float32, jnp.log(3e-05), jnp.log(0.00015)))
    tail_sign = jnp.where(jax.random.uniform(derived_seeds[6], (D,), jnp.float32) < 0.5, -1.0, 1.0)
    tail_shape = jax.random.uniform(derived_seeds[7], (NUCLEOTIDE_COUNT, D), jnp.float32, 0.0, 2.0)
    decaying = stochastic_jitter * jnp.sqrt(2.0 * decay_speed) * jnp.exp(-decay_speed * nucleotide_offset)
    lasting = (tail_sign * tail_size)[None, :] * tail_shape
    return (decaying + lasting) * clustered_erasure


def draw_values(key, part):
    key = jax.random.fold_in(key, 11)
    derived_seeds = jax.random.split(key, 3)
    noise = jax.random.truncated_normal(derived_seeds[0], -5.0, 5.0, (NUCLEOTIDE_COUNT, D), jnp.float32)
    level = jax.random.uniform(derived_seeds[1], (D,), jnp.float32, 0.3, 0.7)
    level_sign = jnp.where(jax.random.uniform(derived_seeds[2], (D,), jnp.float32) < 0.5, -1.0, 1.0)
    return (noise + (level_sign * level)[None, :]).astype(jnp.bfloat16)


def touch_ends(result, key, smallest, top_value):
    spot = [jax.random.randint(jax.random.fold_in(key, axis), (), 0, length) for axis, length in enumerate(result.shape)]
    longest = result.shape.index(max(result.shape))
    beside = spot[:longest] + [(spot[longest] + 1) % result.shape[longest]] + spot[longest + 1:]
    return result.at[tuple(spot)].set(smallest).at[tuple(beside)].set(top_value)


def levels(key, extent, cuts, least, largest):
    loudness = 1.0
    for position, shards_of in cuts:
        steps = jax.random.uniform(jax.random.fold_in(jax.random.fold_in(key, 6), position), (shards_of,), jnp.float32, least / len(cuts), largest / len(cuts))
        loudness = loudness * jnp.repeat(jnp.exp(steps), extent[position] // shards_of).reshape((-1,) + (1,) * (len(extent) - 1 - position))
    return loudness


def normal_values(own_key, shape, scale, bound, cuts=(), kind=jnp.bfloat16):
    array = jax.random.normal(own_key, shape, jnp.float32) * scale
    if len(cuts) > 0:
        array = levels(own_key, shape, cuts, -0.22, 0.18) * array
    return jnp.clip(array, min=-bound, max=bound).astype(kind)


def setup_inputs(seed: int = 0) -> dict:
    keys = jax.random.split(jax.random.key(seed), 7)
    values = draw_values(jax.random.fold_in(keys[6], 71), 0)
    gates = normal_values(keys[1], (NUCLEOTIDE_COUNT, D), 1.0, 6.0, ((0, 64), (1, 4)))
    filters = draw_filters(jax.random.fold_in(keys[6], 71), 0)
    skip = normal_values(keys[3], (D,), 1.0, 4.0, ((0, 4),), jnp.float32)
    cotangent = normal_values(keys[4], (NUCLEOTIDE_COUNT, D), 1.0, 6.0, ((0, 64), (1, 4)))
    flagged = touch_ends((jax.random.randint(keys[5], (NUCLEOTIDE_COUNT,), 0, 2) < 1).astype(jnp.int32), jax.random.fold_in(keys[5], 1), 0, 1)
    return dict(values=values, gates=gates, filters=filters, skip=skip, cotangent=cotangent, flagged=flagged)


def reference(values, gates, filters, skip, cotangent, flagged):
    length = values.shape[0]
    padded = 2 * length
    scale = NUCLEOTIDE_COUNT ** -0.5
    value_rows = values.astype(jnp.float32)
    gate_rows = gates.astype(jnp.float32)
    value_spec = jnp.fft.rfft(value_rows, n=padded, axis=0)
    filter_spec = jnp.fft.rfft(filters, n=padded, axis=0)
    kernel = filter_spec + jnp.conj(filter_spec[:, ::-1])
    mixing = jnp.fft.irfft(kernel * value_spec, n=padded, axis=0)[:length] + skip[None, :] * value_rows
    mixed = (gate_rows * mixing).astype(jnp.bfloat16)
    masked = cotangent.astype(jnp.float32) * flagged.astype(jnp.float32)[:, None]
    gate_grad = (masked * mixing).astype(jnp.bfloat16)
    inner_grad = gate_rows * masked
    inner_spec = jnp.fft.rfft(inner_grad, n=padded, axis=0)
    value_grad = jnp.fft.irfft(jnp.conj(kernel) * inner_spec, n=padded, axis=0)[:length]
    value_grad = (value_grad + skip[None, :] * inner_grad).astype(jnp.bfloat16)
    product = jnp.conj(value_spec) * inner_spec
    filter_grad = jnp.fft.irfft(product + jnp.conj(product[:, ::-1]), n=padded, axis=0)[:length] * scale
    skip_grad = jnp.sum(value_rows * inner_grad, axis=0) * scale
    return mixed, value_grad, gate_grad, filter_grad, skip_grad
```

```python
import functools
import math

import jax
import jax.numpy as jnp
import ml_dtypes
import numpy as np
from jax import lax
from jax.experimental import pallas as pl
from jax.experimental.pallas import tpu as pltpu
from jax.sharding import PartitionSpec as P

MESH = pl.DeviceIdType.MESH
F32 = jnp.float32
BF16 = jnp.bfloat16
SEQ = 64
SIDE = 128
GROUPS = 128


def halves(table):
    high = table.astype(ml_dtypes.bfloat16)
    low = (table - high.astype(np.float64)).astype(ml_dtypes.bfloat16)
    return high, low


def tables():
    freq = np.arange(SIDE)
    coarse = np.arange(SIDE)
    order = np.concatenate([2 * np.arange(SEQ), 2 * np.arange(SEQ) + 1])
    angle = 2 * math.pi * ((2 * freq[:, None] + 1) * order[None, :] % 512) / 512
    first = np.concatenate([np.cos(angle), -np.sin(angle)], axis=0)
    first_hi, first_lo = halves(first)
    first_in = np.concatenate([first_hi, first_hi, first_lo], axis=1)
    last_hi, last_lo = halves(first.T * 2.0**-14)
    last_out = np.concatenate([last_hi, last_hi, last_lo], axis=1)
    turn = 2 * math.pi * ((2 * freq[:, None] + 1) * coarse[None, :]) / 65536
    angle = 2 * math.pi * (coarse[:, None] * coarse[None, :] % SIDE) / SIDE
    cosine, sine = np.cos(angle), np.sin(angle)
    second = np.block([[cosine, -sine], [sine, cosine]])
    second_in = np.concatenate([halves(second)[0]] * 2 + [halves(second)[1]], axis=0)
    second_out = np.concatenate([halves(second.T)[0]] * 2 + [halves(second.T)[1]], axis=0)
    return (
        first_in,
        last_out,
        np.cos(turn).astype(np.float32),
        np.sin(turn).astype(np.float32),
        second_in,
        second_out,
    )


def split(array):
    high = array.astype(BF16)
    return high, (array - high.astype(F32)).astype(BF16)


def dot(left, right):
    return jnp.dot(left, right, preferred_element_type=F32)


def second_step(parts, table):
    high, low = split(jnp.concatenate(parts, axis=0))
    return dot(jnp.concatenate([high, low, high], axis=1), table)


def rotate(both, cosine, sine):
    turned = []
    for side in range(2):
        real = both[:SIDE, side * SIDE : (side + 1) * SIDE]
        imag = both[SIDE:, side * SIDE : (side + 1) * SIDE]
        turned.append(
            jnp.concatenate([real * cosine + imag * sine, imag * cosine - real * sine], axis=1)
        )
    return turned


def rotate_back(both, cosine, sine):
    real, imag = both[:, :SIDE], both[:, SIDE:]
    return real * cosine - imag * sine, imag * cosine + real * sine


def times(left, right):
    lr, li, rr, ri = left[:, :SIDE], left[:, SIDE:], right[:, :SIDE], right[:, SIDE:]
    return jnp.concatenate([lr * rr - li * ri, lr * ri + li * rr], axis=1)


def conj_times(left, right):
    lr, li, rr, ri = left[:, :SIDE], left[:, SIDE:], right[:, :SIDE], right[:, SIDE:]
    return jnp.concatenate([lr * rr + li * ri, lr * ri - li * rr], axis=1)


def add_conj(left, right):
    return jnp.concatenate(
        [left[:, :SIDE] + right[:, :SIDE], left[:, SIDE:] - right[:, SIDE:]], axis=1
    )


def conj(array):
    return jnp.concatenate([array[:, :SIDE], -array[:, SIDE:]], axis=1)


def kernel(
    values, gates, filters, skip, cotangent, flagged,
    first_in, last_out, cosine, sine, second_in, second_out,
    mixed, value_grad, gate_grad, filter_grad, skip_grad,
    send_fv, send_w, recv_fv, recv_w,
    back_mix, back_vg, back_fg, back_skip,
    ret_mix, ret_vg, ret_fg, ret_skip,
    inner, kept_k, kept_v, send_sem, recv_sem,
):
    seq = lax.axis_index("seq")
    ch = lax.axis_index("ch")
    outer = (ch == 0) | (ch == 3)
    mirror = ch // 2

    owner_ch = [jnp.where(outer, 1, 0), jnp.where(outer, 2, 3)]
    group_sign = 1 - 2 * mirror
    group_base = 127 * mirror
    home_ch = [jnp.where(outer, 1, 0), jnp.where(outer, 2, 3)]
    mine = seq + SEQ * mirror

    x, y, rest = seq // 16, seq // 4 % 4, seq % 4
    along_x = [(x + step) % 4 * 16 for step in range(4)]
    along_y = [(y + step) % 4 * 4 for step in range(4)]

    def peers(visit):
        def some(step, carry):
            half = step % 2
            there = (rest + step // 2) % 4
            for px in along_x:
                for py in along_y:
                    visit(px + py + there, half)
            return carry

        lax.fori_loop(0, 8, some, 0)

    barrier = pltpu.get_barrier_semaphore()

    def greet(there, half):
        pl.semaphore_signal(
            barrier,
            inc=1,
            device_id=(there, jnp.where(half == 0, owner_ch[0], owner_ch[1])),
            device_id_type=MESH,
        )

    peers(greet)

    def to_owner(src, dst, which):
        def visit(there, half):
            group = group_base + group_sign * (half * SEQ + there)
            pltpu.make_async_remote_copy(
                src_ref=src.at[group // 2, group % 2],
                dst_ref=dst.at[mirror * SEQ + seq],
                send_sem=send_sem.at[which],
                recv_sem=recv_sem.at[which],
                device_id=(there, jnp.where(half == 0, owner_ch[0], owner_ch[1])),
                device_id_type=MESH,
            ).start()

        peers(visit)

    def to_home(src, dst, which):
        def visit(there, half):
            group = jnp.where(half == 0, mine, 127 - mine)
            pltpu.make_async_remote_copy(
                src_ref=src.at[half * SEQ + there],
                dst_ref=dst.at[group // 2, group % 2],
                send_sem=send_sem.at[which],
                recv_sem=recv_sem.at[which],
                device_id=(there, jnp.where(half == 0, home_ch[0], home_ch[1])),
                device_id_type=MESH,
            ).start()

        peers(visit)

    def skips_home(which):
        def visit(there, half):
            group = jnp.where(half == 0, mine, 127 - mine)
            pltpu.make_async_remote_copy(
                src_ref=back_skip.at[half],
                dst_ref=ret_skip.at[group],
                send_sem=send_sem.at[which],
                recv_sem=recv_sem.at[which],
                device_id=(there, jnp.where(half == 0, home_ch[0], home_ch[1])),
                device_id_type=MESH,
            ).start()

        peers(visit)

    def wait_for(semaphores, which, ref):
        pltpu.make_async_copy(ref, ref, semaphores.at[which]).wait()

    rows = lax.broadcasted_iota(jnp.int32, (16, 8, SIDE), 1) < 4

    def block(half, part):
        return pl.ds(half * SIDE, SIDE), pl.ds(part * SIDE, SIDE)

    def pack(top, bottom):
        top, bottom = top.reshape(16, 8, SIDE), bottom.reshape(16, 8, SIDE)
        even = jnp.where(rows, top, pltpu.roll(bottom, 4, 1))
        odd = jnp.where(rows, pltpu.roll(top, 4, 1), bottom)
        return even, odd

    def unpack(even, odd):
        top = jnp.where(rows, even, pltpu.roll(odd, 4, 1))
        bottom = jnp.where(rows, pltpu.roll(even, 4, 1), odd)
        return top.reshape(SIDE, SIDE), bottom.reshape(SIDE, SIDE)

    flags = [
        jnp.broadcast_to(flagged[half : half + 1, :].astype(F32), (SIDE, SIDE)).T
        for half in range(2)
    ]

    for part in range(4):
        here = pl.ds(part * 16, 16)
        for which, source in enumerate((filters, values)):
            turned = [source[block(half, part)].astype(F32).T for half in range(2)]
            send_fv[here, 0, which], send_fv[here, 1, which] = pack(*turned)
    for part in range(4):
        here = pl.ds(part * 16, 16)
        turned = []
        for half in range(2):
            at = block(half, part)
            product = gates[at].astype(F32) * (cotangent[at].astype(F32) * flags[half])
            inner[at] = product
            turned.append(product.T)
        send_w[here, 0], send_w[here, 1] = pack(*turned)

    pl.semaphore_wait(barrier, 128)
    to_owner(send_fv, recv_fv, 0)
    to_owner(send_w, recv_w, 1)

    cos_turn, sin_turn = cosine[...], sine[...]

    def load(flat, start, stride):
        return jnp.concatenate(
            [flat[pl.ds(start + 4 * half, SEQ, stride=stride), :] for half in range(2)], axis=0
        )

    def load_pair(ref, which, count, pair):
        flat = ref.reshape(2 * SEQ * count * 8, SIDE)
        stride = count * 8
        first = load(flat, which * 8 + pair, stride)
        second = load(flat, SEQ * stride + which * 8 + 3 - pair, stride)
        return jnp.concatenate([first, second], axis=1)

    def store_pair(ref, pair, result):
        flat = ref.reshape(2 * SEQ * 8, SIDE)
        for half in range(2):
            top = result[half * SEQ : (half + 1) * SEQ]
            flat[pl.ds(4 * half + pair, SEQ, stride=8), :] = top[:, :SIDE]
            flat[pl.ds(SEQ * 8 + 4 * half + 3 - pair, SEQ, stride=8), :] = top[:, SIDE:]

    def first_step(signal):
        high, low = split(signal)
        return dot(first_in[...], jnp.concatenate([high, low, high], axis=0))

    def first_step_exact(signal):
        high = signal.astype(BF16)
        return dot(first_in[:, SIDE:], jnp.concatenate([high, high], axis=0))

    def inverse(first, second):
        both = second_step([first, second], second_out[...])
        r0, i0 = rotate_back(both[:SIDE], cos_turn, sin_turn)
        r1, i1 = rotate_back(both[SIDE:], cos_turn, sin_turn)
        stacked = jnp.concatenate(
            [jnp.concatenate([r0, r1], axis=1), jnp.concatenate([i0, i1], axis=1)], axis=0
        )
        high, low = split(stacked)
        return dot(last_out[...], jnp.concatenate([high, low, high], axis=0))

    wait_for(recv_sem, 0, recv_fv)
    for pair in range(4):
        f_parts = rotate(first_step(load_pair(recv_fv, 0, 2, pair)), cos_turn, sin_turn)
        v_parts = rotate(first_step_exact(load_pair(recv_fv, 1, 2, pair)), cos_turn, sin_turn)
        spectra = second_step(f_parts + v_parts, second_in[...])
        f0, f1, v0, v1 = (spectra[i * SIDE : (i + 1) * SIDE] for i in range(4))
        k = add_conj(f0, f1)
        kept_k[pair] = k
        kept_v[pair, 0] = v0
        kept_v[pair, 1] = v1
        store_pair(back_mix, pair, inverse(times(k, v0), conj_times(k, v1)))
    to_home(back_mix, ret_mix, 2)

    wait_for(recv_sem, 1, recv_w)
    lanes = lax.broadcasted_iota(jnp.int32, (1, SIDE), 1)
    skip_rows = [jnp.zeros((1, SIDE), F32), jnp.zeros((1, SIDE), F32)]
    for pair in range(4):
        signal = load_pair(recv_w, 0, 1, pair)
        sums = jnp.sum(signal * load_pair(recv_fv, 1, 2, pair), axis=0, keepdims=True)
        for side, group, row in ((0, mine, pair), (1, 127 - mine, 3 - pair)):
            total = jnp.sum(sums[:, side * SIDE : (side + 1) * SIDE], axis=1, keepdims=True)
            skip_rows[side] += jnp.where(lanes == group % 32 * 4 + row, total, 0.0)
        spectra = second_step(rotate(first_step(signal), cos_turn, sin_turn), second_in[...])
        w0, w1 = spectra[:SIDE], spectra[SIDE:]
        k = kept_k[pair]
        store_pair(back_vg, pair, inverse(conj_times(k, w0), times(k, w1)))
        product = add_conj(conj_times(kept_v[pair, 0], w0), conj_times(kept_v[pair, 1], w1))
        store_pair(back_fg, pair, inverse(product, conj(product)))
    back_skip[0] = skip_rows[0]
    back_skip[1] = skip_rows[1]
    to_home(back_vg, ret_vg, 3)
    to_home(back_fg, ret_fg, 4)
    skips_home(5)

    def returned(ref, part):
        here = pl.ds(part * 16, 16)
        top, bottom = unpack(ref[here, 0], ref[here, 1])
        return top.T, bottom.T

    wait_for(recv_sem, 2, ret_mix)
    for part in range(4):
        for half, result in enumerate(returned(ret_mix, part)):
            at = block(half, part)
            result = result + skip[:, at[1]] * values[at].astype(F32)
            mixed[at] = (gates[at].astype(F32) * result).astype(BF16)
            gate_grad[at] = (cotangent[at].astype(F32) * flags[half] * result).astype(BF16)
    wait_for(recv_sem, 3, ret_vg)
    for part in range(4):
        for half, result in enumerate(returned(ret_vg, part)):
            at = block(half, part)
            value_grad[at] = (result + skip[:, at[1]] * inner[at]).astype(BF16)
    wait_for(recv_sem, 4, ret_fg)
    for part in range(4):
        for half, result in enumerate(returned(ret_fg, part)):
            filter_grad[block(half, part)] = result * 2.0**-7
    wait_for(recv_sem, 5, ret_skip)
    for part in range(4):
        skip_grad[part : part + 1, :] = jnp.sum(ret_skip[pl.ds(part * 32, 32)], axis=0) * 2.0**-7

    for which, ref in enumerate((recv_fv, recv_w, ret_mix, ret_vg, ret_fg, ret_skip)):
        wait_for(send_sem, which, ref)


def body(values, gates, filters, skip, cotangent, flagged):
    constants = [jnp.asarray(table) for table in tables()]
    bases, width = values.shape
    vmem = pl.BlockSpec(memory_space=pltpu.VMEM)

    def scratch(*shape):
        return pltpu.VMEM(shape, F32)

    outs = pl.pallas_call(
        kernel,
        out_shape=[
            jax.ShapeDtypeStruct((bases, width), BF16),
            jax.ShapeDtypeStruct((bases, width), BF16),
            jax.ShapeDtypeStruct((bases, width), BF16),
            jax.ShapeDtypeStruct((bases, width), F32),
            jax.ShapeDtypeStruct((4, SIDE), F32),
        ],
        in_specs=[vmem] * 12,
        out_specs=[vmem] * 5,
        scratch_shapes=[
            scratch(64, 2, 2, 8, SIDE),
            scratch(64, 2, 8, SIDE),
            scratch(GROUPS, 2, 8, SIDE),
            scratch(GROUPS, 8, SIDE),
            scratch(GROUPS, 8, SIDE),
            scratch(GROUPS, 8, SIDE),
            scratch(GROUPS, 8, SIDE),
            scratch(2, 1, SIDE),
            scratch(64, 2, 8, SIDE),
            scratch(64, 2, 8, SIDE),
            scratch(64, 2, 8, SIDE),
            scratch(GROUPS, 1, SIDE),
            scratch(bases, width),
            scratch(4, SIDE, 2 * SIDE),
            scratch(4, 2, SIDE, 2 * SIDE),
            pltpu.SemaphoreType.DMA((6,)),
            pltpu.SemaphoreType.DMA((6,)),
        ],
        compiler_params=pltpu.CompilerParams(
            collective_id=0, has_side_effects=True, vmem_limit_bytes=48 << 20
        ),
        name="hyena",
    )(values, gates, filters, skip.reshape(1, width), cotangent, flagged.reshape(2, SIDE), *constants)
    return (*outs[:4], outs[4].reshape(width))


def solution(mesh):
    placed = (P("seq", "ch"), P("seq", "ch"), P("seq", "ch"), P("ch"), P("seq", "ch"), P("seq"))
    return jax.shard_map(
        body,
        mesh=mesh,
        in_specs=placed,
        out_specs=(P("seq", "ch"), P("seq", "ch"), P("seq", "ch"), P("seq", "ch"), P("ch")),
        check_vma=False,
    )
```

```python
import functools
import math

import jax
import jax.numpy as jnp
import ml_dtypes
import numpy as np
from jax import lax
from jax.experimental import pallas as pl
from jax.experimental.pallas import tpu as pltpu
from jax.sharding import PartitionSpec as P

MESH = pl.DeviceIdType.MESH
F32 = jnp.float32
BF16 = jnp.bfloat16
SEQ = 64
SIDE = 128
GROUPS = 128


def halves(table):
    high = table.astype(ml_dtypes.bfloat16)
    low = (table - high.astype(np.float64)).astype(ml_dtypes.bfloat16)
    return high, low


def tables():
    freq = np.arange(SIDE)
    coarse = np.arange(SIDE)
    order = np.concatenate([2 * np.arange(SEQ), 2 * np.arange(SEQ) + 1])
    angle = 2 * math.pi * ((2 * freq[:, None] + 1) * order[None, :] % 512) / 512
    first = np.concatenate([np.cos(angle), -np.sin(angle)], axis=0)
    first_hi, first_lo = halves(first)
    first_in = np.concatenate([first_hi, first_hi, first_lo], axis=1)
    last_hi, last_lo = halves(first.T * 2.0**-14)
    last_out = np.concatenate([last_hi, last_hi, last_lo], axis=1)
    turn = 2 * math.pi * ((2 * freq[:, None] + 1) * coarse[None, :]) / 65536
    angle = 2 * math.pi * (coarse[:, None] * coarse[None, :] % SIDE) / SIDE
    cosine, sine = np.cos(angle), np.sin(angle)
    second = np.block([[cosine, -sine], [sine, cosine]])
    second_in = np.concatenate([halves(second)[0]] * 2 + [halves(second)[1]], axis=0)
    second_out = np.concatenate([halves(second.T)[0]] * 2 + [halves(second.T)[1]], axis=0)
    return (
        first_in,
        last_out,
        np.cos(turn).astype(np.float32),
        np.sin(turn).astype(np.float32),
        second_in,
        second_out,
    )


def split(array):
    high = array.astype(BF16)
    return high, (array - high.astype(F32)).astype(BF16)


def dot(left, right):
    return jnp.dot(left, right, preferred_element_type=F32)


def second_step(parts, table):
    high, low = split(jnp.concatenate(parts, axis=0))
    return dot(jnp.concatenate([high, low, high], axis=1), table)


def rotate(both, cosine, sine):
    turned = []
    for side in range(2):
        real = both[:SIDE, side * SIDE : (side + 1) * SIDE]
        imag = both[SIDE:, side * SIDE : (side + 1) * SIDE]
        turned.append(
            jnp.concatenate([real * cosine + imag * sine, imag * cosine - real * sine], axis=1)
        )
    return turned


def rotate_back(both, cosine, sine):
    real, imag = both[:, :SIDE], both[:, SIDE:]
    return real * cosine - imag * sine, imag * cosine + real * sine


def times(left, right):
    lr, li, rr, ri = left[:, :SIDE], left[:, SIDE:], right[:, :SIDE], right[:, SIDE:]
    return jnp.concatenate([lr * rr - li * ri, lr * ri + li * rr], axis=1)


def conj_times(left, right):
    lr, li, rr, ri = left[:, :SIDE], left[:, SIDE:], right[:, :SIDE], right[:, SIDE:]
    return jnp.concatenate([lr * rr + li * ri, lr * ri - li * rr], axis=1)


def add_conj(left, right):
    return jnp.concatenate(
        [left[:, :SIDE] + right[:, :SIDE], left[:, SIDE:] - right[:, SIDE:]], axis=1
    )


def conj(array):
    return jnp.concatenate([array[:, :SIDE], -array[:, SIDE:]], axis=1)


def kernel(
    values_hbm, gates_hbm, filters_hbm, skip_hbm, cotangent_hbm, flagged_hbm,
    first_in_hbm, last_out_hbm, cosine_hbm, sine_hbm, second_in_hbm, second_out_hbm,
    mixed, value_grad, gate_grad, ret_fg, skip_grad,
    values, gates, filters, skip, cotangent, flagged,
    first_in, last_out, cosine, sine, second_in, second_out,
    send_f, send_v, send_w, recv_f, recv_v, recv_w,
    back_mix, back_vg, back_fg, ret_mix, ret_vg,
    inner, kept_k, kept_v, kept_w, sums,
    send_sem, recv_sem, sums_send, sums_recv, fetch_sem,
):
    fetches = [
        pltpu.make_async_copy(src, dst, fetch_sem.at[i])
        for i, (src, dst) in enumerate(
            (
                (filters_hbm, filters),
                (values_hbm, values),
                (gates_hbm, gates),
                (cotangent_hbm, cotangent),
                (flagged_hbm, flagged),
                (skip_hbm, skip),
                (first_in_hbm, first_in),
                (last_out_hbm, last_out),
                (cosine_hbm, cosine),
                (sine_hbm, sine),
                (second_in_hbm, second_in),
                (second_out_hbm, second_out),
            )
        )
    ]
    fetches[0].start()

    seq = lax.axis_index("seq")
    ch = lax.axis_index("ch")
    outer = (ch == 0) | (ch == 3)
    mirror = ch // 2

    peer_ch = [jnp.where(outer, 1, 0), jnp.where(outer, 2, 3)]
    group_sign = 1 - 2 * mirror
    group_base = 127 * mirror
    mine = seq + SEQ * mirror

    x, y, rest = seq // 16, seq // 4 % 4, seq % 4
    along_x = [(x + step) % 4 * 16 for step in range(4)]
    along_y = [(y + step) % 4 * 4 for step in range(4)]

    def peers(visit):
        def some(step, carry):
            turn = (step + seq + 3 * ch) % 8
            there = [(rest + turn // 2 + k) % 4 for k in range(4)]
            even = turn % 2
            sides = [
                (even, jnp.where(even == 0, peer_ch[0], peer_ch[1])),
                (1 - even, jnp.where(even == 0, peer_ch[1], peer_ch[0])),
            ]
            for k in range(16):
                visit(along_x[k % 4] + along_y[k // 4] + there[(k + k // 4) % 4], *sides[k % 2])
            return carry

        lax.fori_loop(0, 8, some, 0)

    barrier = pltpu.get_barrier_semaphore()

    def greet(there, half, ch_there):
        pl.semaphore_signal(barrier, inc=1, device_id=(there, ch_there), device_id_type=MESH)

    circles = [
        (x, [along_x[k] + seq % 16 for k in range(1, 4)]),
        (y, [x * 16 + along_y[k] + rest for k in range(1, 4)]),
        (rest, [seq - rest + (rest + k) % 4 for k in range(1, 4)]),
    ]

    peers(greet)
    for _, others in circles:
        for there in others:
            pl.semaphore_signal(barrier, inc=1, device_id=(there, ch), device_id_type=MESH)
    for fetch in fetches[1:]:
        fetch.start()

    def remote(src, dst, which, there, ch_there):
        pltpu.make_async_remote_copy(
            src_ref=src,
            dst_ref=dst,
            send_sem=send_sem.at[which],
            recv_sem=recv_sem.at[which],
            device_id=(there, ch_there),
            device_id_type=MESH,
        ).start()

    def to_owner(src, dst, which):
        def visit(there, half, ch_there):
            group = group_base + group_sign * (half * SEQ + there)
            remote(src.at[group // 2, group % 2], dst.at[mirror * SEQ + seq], which, there, ch_there)

        peers(visit)

    def to_home(src, dst, which):
        def visit(there, half, ch_there):
            group = mine + half * (127 - 2 * mine)
            remote(src.at[half * SEQ + there], dst.at[group // 2, group % 2], which, there, ch_there)

        peers(visit)

    def wait_for(semaphores, which, ref):
        pltpu.make_async_copy(ref, ref, semaphores.at[which]).wait()

    def send_sums(stage, total):
        place, others = circles[stage]
        sums[stage, place] = total
        for there in others:
            pltpu.make_async_remote_copy(
                src_ref=sums.at[stage, place],
                dst_ref=sums.at[stage, place],
                send_sem=sums_send.at[stage],
                recv_sem=sums_recv.at[stage],
                device_id=(there, ch),
                device_id_type=MESH,
            ).start()

    def summed(stage):
        wait_for(sums_recv, stage, sums.at[stage, pl.ds(0, 3)])
        wait_for(sums_send, stage, sums.at[stage, pl.ds(0, 3)])
        return (sums[stage, 0] + sums[stage, 1]) + (sums[stage, 2] + sums[stage, 3])

    rows = lax.broadcasted_iota(jnp.int32, (16, 8, SIDE), 1) < 4

    def block(half, part):
        return pl.ds(half * SIDE, SIDE), pl.ds(part * SIDE, SIDE)

    def pack(top, bottom):
        top, bottom = top.reshape(16, 8, SIDE), bottom.reshape(16, 8, SIDE)
        even = jnp.where(rows, top, pltpu.roll(bottom, 4, 1))
        odd = jnp.where(rows, pltpu.roll(top, 4, 1), bottom)
        return even, odd

    def unpack(even, odd):
        top = jnp.where(rows, even, pltpu.roll(odd, 4, 1))
        bottom = jnp.where(rows, pltpu.roll(even, 4, 1), odd)
        return top.reshape(SIDE, SIDE), bottom.reshape(SIDE, SIDE)

    def pack_all(source, dst):
        for part in range(4):
            here = pl.ds(part * 16, 16)
            turned = [source[block(half, part)].astype(F32).T for half in range(2)]
            dst[here, 0], dst[here, 1] = pack(*turned)

    fetches[0].wait()
    pack_all(filters, send_f)
    pl.semaphore_wait(barrier, 137)
    to_owner(send_f, recv_f, 0)
    fetches[1].wait()
    pack_all(values, send_v)
    to_owner(send_v, recv_v, 1)

    for fetch in fetches[2:]:
        fetch.wait()
    flags = [
        jnp.broadcast_to(flagged[half : half + 1, :].astype(F32), (SIDE, SIDE)).T
        for half in range(2)
    ]
    totals = []
    for part in range(4):
        here = pl.ds(part * 16, 16)
        turned = []
        total = jnp.zeros((1, SIDE), F32)
        for half in range(2):
            at = block(half, part)
            product = gates[at].astype(F32) * (cotangent[at].astype(F32) * flags[half])
            inner[at] = product
            turned.append(product.T)
            total += jnp.sum(values[at].astype(F32) * product, axis=0, keepdims=True)
        send_w[here, 0], send_w[here, 1] = pack(*turned)
        totals.append(total)
    send_sums(0, jnp.concatenate(totals, axis=0))
    to_owner(send_w, recv_w, 2)

    cos_turn, sin_turn = cosine[...], sine[...]

    def load_pair(ref, pair):
        flat = ref.reshape(2 * SEQ * 8, SIDE)
        first = [flat[pl.ds(4 * half + pair, SEQ, stride=8), :] for half in range(2)]
        second = [
            flat[pl.ds(SEQ * 8 + 4 * half + 3 - pair, SEQ, stride=8), :] for half in range(2)
        ]
        return jnp.concatenate(
            [jnp.concatenate(first, axis=0), jnp.concatenate(second, axis=0)], axis=1
        )

    def store_pair(ref, pair, result):
        flat = ref.reshape(2 * SEQ * 8, SIDE)
        for half in range(2):
            top = result[half * SEQ : (half + 1) * SEQ]
            flat[pl.ds(4 * half + pair, SEQ, stride=8), :] = top[:, :SIDE]
            flat[pl.ds(SEQ * 8 + 4 * half + 3 - pair, SEQ, stride=8), :] = top[:, SIDE:]

    def first_step(signal):
        high, low = split(signal)
        return dot(first_in[...], jnp.concatenate([high, low, high], axis=0))

    def first_step_exact(signal):
        high = signal.astype(BF16)
        return dot(first_in[:, SIDE:], jnp.concatenate([high, high], axis=0))

    def spectra(stepped):
        both = second_step(rotate(stepped, cos_turn, sin_turn), second_in[...])
        return both[:SIDE], both[SIDE:]

    def inverse(first, second):
        both = second_step([first, second], second_out[...])
        r0, i0 = rotate_back(both[:SIDE], cos_turn, sin_turn)
        r1, i1 = rotate_back(both[SIDE:], cos_turn, sin_turn)
        stacked = jnp.concatenate(
            [jnp.concatenate([r0, r1], axis=1), jnp.concatenate([i0, i1], axis=1)], axis=0
        )
        high, low = split(stacked)
        return dot(last_out[...], jnp.concatenate([high, low, high], axis=0))

    wait_for(recv_sem, 0, recv_f)
    for pair in range(4):
        kept_k[pair] = add_conj(*spectra(first_step(load_pair(recv_f, pair))))
    wait_for(recv_sem, 1, recv_v)
    for pair in range(4):
        v0, v1 = spectra(first_step_exact(load_pair(recv_v, pair)))
        kept_v[pair, 0], kept_v[pair, 1] = v0, v1
        k = kept_k[pair]
        store_pair(back_mix, pair, inverse(times(k, v0), conj_times(k, v1)))
    to_home(back_mix, ret_mix, 3)
    send_sums(1, summed(0))

    wait_for(recv_sem, 2, recv_w)
    for pair in range(4):
        w0, w1 = spectra(first_step(load_pair(recv_w, pair)))
        kept_w[pair, 0], kept_w[pair, 1] = w0, w1
        k = kept_k[pair]
        store_pair(back_vg, pair, inverse(conj_times(k, w0), times(k, w1)))
    to_home(back_vg, ret_vg, 4)
    send_sums(2, summed(1))
    for pair in range(4):
        product = add_conj(
            conj_times(kept_v[pair, 0], kept_w[pair, 0]),
            conj_times(kept_v[pair, 1], kept_w[pair, 1]),
        )
        store_pair(back_fg, pair, inverse(product, conj(product)))
    to_home(back_fg, ret_fg, 5)

    def returned(ref, part):
        here = pl.ds(part * 16, 16)
        top, bottom = unpack(ref[here, 0], ref[here, 1])
        return top.T, bottom.T

    wait_for(recv_sem, 3, ret_mix)
    for part in range(4):
        for half, result in enumerate(returned(ret_mix, part)):
            at = block(half, part)
            result = result + skip[:, at[1]] * values[at].astype(F32)
            mixed[at] = (gates[at].astype(F32) * result).astype(BF16)
            gate_grad[at] = (cotangent[at].astype(F32) * flags[half] * result).astype(BF16)
    skip_grad[...] = summed(2) * 2.0**-7
    wait_for(recv_sem, 4, ret_vg)
    for part in range(4):
        for half, result in enumerate(returned(ret_vg, part)):
            at = block(half, part)
            value_grad[at] = (result + skip[:, at[1]] * inner[at]).astype(BF16)
    for which, ref in enumerate((recv_f, recv_v, recv_w, ret_mix, ret_vg, ret_fg)):
        wait_for(send_sem, which, ref)
    wait_for(recv_sem, 5, ret_fg)


def finish(*refs):
    arrived, outs, (turned, out_sem) = refs[:5], refs[5:10], refs[10:]
    stores = [
        pltpu.make_async_copy(src, dst, out_sem.at[i])
        for i, (src, dst) in enumerate(zip((*arrived[:3], turned, arrived[4]), outs))
    ]
    for i in (0, 1, 2, 4):
        stores[i].start()
    ret_fg = arrived[3]
    rows = lax.broadcasted_iota(jnp.int32, (16, 8, SIDE), 1) < 4
    for part in range(4):
        even, odd = ret_fg[pl.ds(part * 16, 16), 0], ret_fg[pl.ds(part * 16, 16), 1]
        top = jnp.where(rows, even, pltpu.roll(odd, 4, 1)).reshape(SIDE, SIDE)
        bottom = jnp.where(rows, pltpu.roll(even, 4, 1), odd).reshape(SIDE, SIDE)
        for half, result in enumerate((top, bottom)):
            turned[pl.ds(half * SIDE, SIDE), pl.ds(part * SIDE, SIDE)] = result.T * 2.0**-7
    stores[3].start()
    for store in stores:
        store.wait()


def body(values, gates, filters, skip, cotangent, flagged):
    constants = [jnp.asarray(table) for table in tables()]
    bases, width = values.shape
    hbm = pl.BlockSpec(memory_space=pltpu.HBM)
    vmem = pl.BlockSpec(memory_space=pltpu.VMEM)

    def scratch(*shape):
        return pltpu.VMEM(shape, F32)

    operands = (values, gates, filters, skip.reshape(1, width), cotangent, flagged.reshape(2, SIDE))
    halfwords = jax.ShapeDtypeStruct((bases, width), BF16)
    home = (GROUPS // 2, 2, 8, SIDE)
    owner = (GROUPS, 8, SIDE)
    outs = pl.pallas_call(
        kernel,
        out_shape=[
            halfwords,
            halfwords,
            halfwords,
            jax.ShapeDtypeStruct(home, F32),
            jax.ShapeDtypeStruct((4, SIDE), F32),
        ],
        in_specs=[hbm] * 12,
        out_specs=[vmem] * 5,
        scratch_shapes=[
            *[pltpu.VMEM(array.shape, array.dtype) for array in (*operands, *constants)],
            *[scratch(*home)] * 3,
            *[scratch(*owner)] * 6,
            *[scratch(*home)] * 2,
            scratch(bases, width),
            scratch(4, SIDE, 2 * SIDE),
            *[scratch(4, 2, SIDE, 2 * SIDE)] * 2,
            scratch(3, 4, 4, SIDE),
            pltpu.SemaphoreType.DMA((6,)),
            pltpu.SemaphoreType.DMA((6,)),
            pltpu.SemaphoreType.DMA((3,)),
            pltpu.SemaphoreType.DMA((3,)),
            pltpu.SemaphoreType.DMA((12,)),
        ],
        compiler_params=pltpu.CompilerParams(
            collective_id=0, has_side_effects=True, vmem_limit_bytes=28 << 20
        ),
        name="hyena",
    )(*[pltpu.with_memory_space_constraint(array, pltpu.HBM) for array in (*operands, *constants)])
    outs = pl.pallas_call(
        finish,
        out_shape=[
            halfwords,
            halfwords,
            halfwords,
            jax.ShapeDtypeStruct((bases, width), F32),
            jax.ShapeDtypeStruct((4, SIDE), F32),
        ],
        in_specs=[vmem] * 5,
        out_specs=[hbm] * 5,
        scratch_shapes=[scratch(bases, width), pltpu.SemaphoreType.DMA((5,))],
        compiler_params=pltpu.CompilerParams(vmem_limit_bytes=28 << 20),
        name="finish",
    )(*outs)
    return (*outs[:4], outs[4].reshape(width))


def solution(mesh):
    placed = (P("seq", "ch"), P("seq", "ch"), P("seq", "ch"), P("ch"), P("seq", "ch"), P("seq"))
    return jax.shard_map(
        body,
        mesh=mesh,
        in_specs=placed,
        out_specs=(P("seq", "ch"), P("seq", "ch"), P("seq", "ch"), P("seq", "ch"), P("ch")),
        check_vma=False,
    )
```

```python
import functools
import math

import jax
import jax.numpy as jnp
import ml_dtypes
import numpy as np
from jax import lax
from jax.experimental import pallas as pl
from jax.experimental.pallas import tpu as pltpu
from jax.sharding import PartitionSpec as P

MESH = pl.DeviceIdType.MESH
F32 = jnp.float32
BF16 = jnp.bfloat16
SEQ = 64
SIDE = 128
GROUPS = 128


def halves(table):
    high = table.astype(ml_dtypes.bfloat16)
    low = (table - high.astype(np.float64)).astype(ml_dtypes.bfloat16)
    return high, low


def tables():
    freq = np.arange(SIDE)
    coarse = np.arange(SIDE)
    order = np.concatenate([2 * np.arange(SEQ), 2 * np.arange(SEQ) + 1])
    angle = 2 * math.pi * ((2 * freq[:, None] + 1) * order[None, :] % 512) / 512
    first = np.concatenate([np.cos(angle), -np.sin(angle)], axis=0)
    first_hi, first_lo = halves(first)
    first_in = np.concatenate([first_hi, first_hi, first_lo], axis=1)
    last_hi, last_lo = halves(first.T * 2.0**-14)
    last_out = np.concatenate([last_hi, last_hi, last_lo], axis=1)
    turn = 2 * math.pi * ((2 * freq[:, None] + 1) * coarse[None, :]) / 65536
    angle = 2 * math.pi * (coarse[:, None] * coarse[None, :] % SIDE) / SIDE
    cosine, sine = np.cos(angle), np.sin(angle)
    second = np.block([[cosine, -sine], [sine, cosine]])
    second_in = np.concatenate([halves(second)[0]] * 2 + [halves(second)[1]], axis=0)
    second_out = np.concatenate([halves(second.T)[0]] * 2 + [halves(second.T)[1]], axis=0)
    return (
        first_in,
        last_out,
        np.cos(turn).astype(np.float32),
        np.sin(turn).astype(np.float32),
        second_in,
        second_out,
    )


def split(array):
    high = array.astype(BF16)
    return high, (array - high.astype(F32)).astype(BF16)


def dot(left, right):
    return jnp.dot(left, right, preferred_element_type=F32)


def second_step(parts, table):
    high, low = split(jnp.concatenate(parts, axis=0))
    return dot(jnp.concatenate([high, low, high], axis=1), table)


def rotate(both, cosine, sine):
    turned = []
    for side in range(2):
        real = both[:SIDE, side * SIDE : (side + 1) * SIDE]
        imag = both[SIDE:, side * SIDE : (side + 1) * SIDE]
        turned.append(
            jnp.concatenate([real * cosine + imag * sine, imag * cosine - real * sine], axis=1)
        )
    return turned


def rotate_back(both, cosine, sine):
    real, imag = both[:, :SIDE], both[:, SIDE:]
    return real * cosine - imag * sine, imag * cosine + real * sine


def times(left, right):
    lr, li, rr, ri = left[:, :SIDE], left[:, SIDE:], right[:, :SIDE], right[:, SIDE:]
    return jnp.concatenate([lr * rr - li * ri, lr * ri + li * rr], axis=1)


def conj_times(left, right):
    lr, li, rr, ri = left[:, :SIDE], left[:, SIDE:], right[:, :SIDE], right[:, SIDE:]
    return jnp.concatenate([lr * rr + li * ri, lr * ri - li * rr], axis=1)


def add_conj(left, right):
    return jnp.concatenate(
        [left[:, :SIDE] + right[:, :SIDE], left[:, SIDE:] - right[:, SIDE:]], axis=1
    )


def conj(array):
    return jnp.concatenate([array[:, :SIDE], -array[:, SIDE:]], axis=1)


def kernel(
    values_hbm, gates_hbm, filters_hbm, skip_hbm, cotangent_hbm, flagged_hbm,
    first_in_hbm, last_out_hbm, cosine_hbm, sine_hbm, second_in_hbm, second_out_hbm,
    mixed, value_grad, gate_grad, ret_fg, skip_grad,
    values, gates, filters, skip, cotangent, flagged,
    first_in, last_out, cosine, sine, second_in, second_out,
    send_fv, send_w, recv_fv, recv_w,
    back_mix, back_vg, back_fg, ret_mix, ret_vg,
    inner, kept_k, kept_v, kept_w, sums,
    send_sem, recv_sem, sums_send, sums_recv, fetch_sem,
):
    fetches = [
        pltpu.make_async_copy(src, dst, fetch_sem.at[i])
        for i, (src, dst) in enumerate(
            (
                (filters_hbm, filters),
                (values_hbm, values),
                (gates_hbm, gates),
                (cotangent_hbm, cotangent),
                (flagged_hbm, flagged),
                (skip_hbm, skip),
                (first_in_hbm, first_in),
                (last_out_hbm, last_out),
                (cosine_hbm, cosine),
                (sine_hbm, sine),
                (second_in_hbm, second_in),
                (second_out_hbm, second_out),
            )
        )
    ]
    fetches[0].start()

    seq = lax.axis_index("seq")
    ch = lax.axis_index("ch")
    outer = (ch == 0) | (ch == 3)
    mirror = ch // 2

    peer_ch = [jnp.where(outer, 1, 0), jnp.where(outer, 2, 3)]
    group_sign = 1 - 2 * mirror
    group_base = 127 * mirror
    mine = seq + SEQ * mirror

    x, y, rest = seq // 16, seq // 4 % 4, seq % 4
    along_x = [(x + step) % 4 * 16 for step in range(4)]
    along_y = [(y + step) % 4 * 4 for step in range(4)]

    along_rest = [(rest + step) % 4 for step in range(4)]

    def peers(visit):
        def some(step, carry):
            far_x = (x + jnp.where(step == 0, 2, jnp.where(step == 3, 0, 2 * step - 1))) % 4 * 16
            for far_y in (2, 1, 3, 0):
                for k in range(8):
                    visit(far_x + along_y[far_y] + along_rest[k % 4], k // 4, peer_ch[k // 4])
            return carry

        lax.fori_loop(0, 4, some, 0)

    barrier = pltpu.get_barrier_semaphore()

    def greet(there, half, ch_there):
        pl.semaphore_signal(barrier, inc=1, device_id=(there, ch_there), device_id_type=MESH)

    circles = [
        (x, [along_x[k] + seq % 16 for k in range(1, 4)]),
        (y, [x * 16 + along_y[k] + rest for k in range(1, 4)]),
        (rest, [seq - rest + (rest + k) % 4 for k in range(1, 4)]),
    ]

    peers(greet)
    for _, others in circles:
        for there in others:
            pl.semaphore_signal(barrier, inc=1, device_id=(there, ch), device_id_type=MESH)
    for fetch in fetches[1:]:
        fetch.start()

    def remote(src, dst, which, there, ch_there):
        pltpu.make_async_remote_copy(
            src_ref=src,
            dst_ref=dst,
            send_sem=send_sem.at[which],
            recv_sem=recv_sem.at[which],
            device_id=(there, ch_there),
            device_id_type=MESH,
        ).start()

    def to_owner(src, dst, which):
        def visit(there, half, ch_there):
            group = group_base + group_sign * (half * SEQ + there)
            remote(src.at[group // 2, group % 2], dst.at[mirror * SEQ + seq], which, there, ch_there)

        peers(visit)

    def to_home(src, dst, which):
        def visit(there, half, ch_there):
            group = mine + half * (127 - 2 * mine)
            remote(src.at[half * SEQ + there], dst.at[group // 2, group % 2], which, there, ch_there)

        peers(visit)

    def wait_for(semaphores, which, ref):
        pltpu.make_async_copy(ref, ref, semaphores.at[which]).wait()

    def send_sums(stage, total):
        place, others = circles[stage]
        sums[stage, place] = total
        for there in others:
            pltpu.make_async_remote_copy(
                src_ref=sums.at[stage, place],
                dst_ref=sums.at[stage, place],
                send_sem=sums_send.at[stage],
                recv_sem=sums_recv.at[stage],
                device_id=(there, ch),
                device_id_type=MESH,
            ).start()

    def summed(stage):
        wait_for(sums_recv, stage, sums.at[stage, pl.ds(0, 3)])
        wait_for(sums_send, stage, sums.at[stage, pl.ds(0, 3)])
        return (sums[stage, 0] + sums[stage, 1]) + (sums[stage, 2] + sums[stage, 3])

    rows = lax.broadcasted_iota(jnp.int32, (16, 8, SIDE), 1) < 4

    def block(half, part):
        return pl.ds(half * SIDE, SIDE), pl.ds(part * SIDE, SIDE)

    def pack(top, bottom):
        top, bottom = top.reshape(16, 8, SIDE), bottom.reshape(16, 8, SIDE)
        even = jnp.where(rows, top, pltpu.roll(bottom, 4, 1))
        odd = jnp.where(rows, pltpu.roll(top, 4, 1), bottom)
        return even, odd

    def unpack(even, odd):
        top = jnp.where(rows, even, pltpu.roll(odd, 4, 1))
        bottom = jnp.where(rows, pltpu.roll(even, 4, 1), odd)
        return top.reshape(SIDE, SIDE), bottom.reshape(SIDE, SIDE)

    def pack_all(source, dst, which):
        for part in range(4):
            here = pl.ds(part * 16, 16)
            turned = [source[block(half, part)].astype(F32).T for half in range(2)]
            dst[here, 0, which], dst[here, 1, which] = pack(*turned)

    fetches[0].wait()
    pack_all(filters, send_fv, 0)
    fetches[1].wait()
    pack_all(values, send_fv, 1)
    pl.semaphore_wait(barrier, 137)
    to_owner(send_fv, recv_fv, 0)

    for fetch in fetches[2:]:
        fetch.wait()
    flags = [
        jnp.broadcast_to(flagged[half : half + 1, :].astype(F32), (SIDE, SIDE)).T
        for half in range(2)
    ]
    totals = []
    for part in range(4):
        here = pl.ds(part * 16, 16)
        turned = []
        total = jnp.zeros((1, SIDE), F32)
        for half in range(2):
            at = block(half, part)
            product = gates[at].astype(F32) * (cotangent[at].astype(F32) * flags[half])
            inner[at] = product
            turned.append(product.T)
            total += jnp.sum(values[at].astype(F32) * product, axis=0, keepdims=True)
        send_w[here, 0], send_w[here, 1] = pack(*turned)
        totals.append(total)
    send_sums(0, jnp.concatenate(totals, axis=0))
    to_owner(send_w, recv_w, 2)

    cos_turn, sin_turn = cosine[...], sine[...]

    def load_pair(ref, pair, which=0, count=1):
        flat = ref.reshape(2 * SEQ * count * 8, SIDE)
        stride = count * 8
        first = [
            flat[pl.ds(which * 8 + 4 * half + pair, SEQ, stride=stride), :] for half in range(2)
        ]
        start = SEQ * stride + which * 8 + 3 - pair
        second = [flat[pl.ds(start + 4 * half, SEQ, stride=stride), :] for half in range(2)]
        return jnp.concatenate(
            [jnp.concatenate(first, axis=0), jnp.concatenate(second, axis=0)], axis=1
        )

    def store_pair(ref, pair, result):
        flat = ref.reshape(2 * SEQ * 8, SIDE)
        for half in range(2):
            top = result[half * SEQ : (half + 1) * SEQ]
            flat[pl.ds(4 * half + pair, SEQ, stride=8), :] = top[:, :SIDE]
            flat[pl.ds(SEQ * 8 + 4 * half + 3 - pair, SEQ, stride=8), :] = top[:, SIDE:]

    def first_step(signal):
        high, low = split(signal)
        return dot(first_in[...], jnp.concatenate([high, low, high], axis=0))

    def first_step_exact(signal):
        high = signal.astype(BF16)
        return dot(first_in[:, SIDE:], jnp.concatenate([high, high], axis=0))

    def spectra(stepped):
        both = second_step(rotate(stepped, cos_turn, sin_turn), second_in[...])
        return both[:SIDE], both[SIDE:]

    def inverse(first, second):
        both = second_step([first, second], second_out[...])
        r0, i0 = rotate_back(both[:SIDE], cos_turn, sin_turn)
        r1, i1 = rotate_back(both[SIDE:], cos_turn, sin_turn)
        stacked = jnp.concatenate(
            [jnp.concatenate([r0, r1], axis=1), jnp.concatenate([i0, i1], axis=1)], axis=0
        )
        high, low = split(stacked)
        return dot(last_out[...], jnp.concatenate([high, low, high], axis=0))

    wait_for(recv_sem, 0, recv_fv)
    for pair in range(4):
        kept_k[pair] = add_conj(*spectra(first_step(load_pair(recv_fv, pair, 0, 2))))
    for pair in range(4):
        v0, v1 = spectra(first_step_exact(load_pair(recv_fv, pair, 1, 2)))
        kept_v[pair, 0], kept_v[pair, 1] = v0, v1
        k = kept_k[pair]
        store_pair(back_mix, pair, inverse(times(k, v0), conj_times(k, v1)))
    to_home(back_mix, ret_mix, 3)
    send_sums(1, summed(0))

    wait_for(recv_sem, 2, recv_w)
    for pair in range(4):
        w0, w1 = spectra(first_step(load_pair(recv_w, pair)))
        kept_w[pair, 0], kept_w[pair, 1] = w0, w1
        k = kept_k[pair]
        store_pair(back_vg, pair, inverse(conj_times(k, w0), times(k, w1)))
    to_home(back_vg, ret_vg, 4)
    send_sums(2, summed(1))
    for pair in range(4):
        product = add_conj(
            conj_times(kept_v[pair, 0], kept_w[pair, 0]),
            conj_times(kept_v[pair, 1], kept_w[pair, 1]),
        )
        store_pair(back_fg, pair, inverse(product, conj(product)))
    to_home(back_fg, ret_fg, 5)

    def returned(ref, part):
        here = pl.ds(part * 16, 16)
        top, bottom = unpack(ref[here, 0], ref[here, 1])
        return top.T, bottom.T

    wait_for(recv_sem, 3, ret_mix)
    for part in range(4):
        for half, result in enumerate(returned(ret_mix, part)):
            at = block(half, part)
            result = result + skip[:, at[1]] * values[at].astype(F32)
            mixed[at] = (gates[at].astype(F32) * result).astype(BF16)
            gate_grad[at] = (cotangent[at].astype(F32) * flags[half] * result).astype(BF16)
    skip_grad[...] = summed(2) * 2.0**-7
    wait_for(recv_sem, 4, ret_vg)
    for part in range(4):
        for half, result in enumerate(returned(ret_vg, part)):
            at = block(half, part)
            value_grad[at] = (result + skip[:, at[1]] * inner[at]).astype(BF16)
    for which, ref in ((0, recv_fv), (2, recv_w), (3, ret_mix), (4, ret_vg), (5, ret_fg)):
        wait_for(send_sem, which, ref)
    wait_for(recv_sem, 5, ret_fg)


def finish(*refs):
    arrived, outs, (turned, out_sem) = refs[:5], refs[5:10], refs[10:]
    stores = [
        pltpu.make_async_copy(src, dst, out_sem.at[i])
        for i, (src, dst) in enumerate(zip((*arrived[:3], turned, arrived[4]), outs))
    ]
    for i in (0, 1, 2, 4):
        stores[i].start()
    ret_fg = arrived[3]
    rows = lax.broadcasted_iota(jnp.int32, (16, 8, SIDE), 1) < 4
    for part in range(4):
        even, odd = ret_fg[pl.ds(part * 16, 16), 0], ret_fg[pl.ds(part * 16, 16), 1]
        top = jnp.where(rows, even, pltpu.roll(odd, 4, 1)).reshape(SIDE, SIDE)
        bottom = jnp.where(rows, pltpu.roll(even, 4, 1), odd).reshape(SIDE, SIDE)
        for half, result in enumerate((top, bottom)):
            turned[pl.ds(half * SIDE, SIDE), pl.ds(part * SIDE, SIDE)] = result.T * 2.0**-7
    stores[3].start()
    for store in stores:
        store.wait()


def body(values, gates, filters, skip, cotangent, flagged):
    constants = [jnp.asarray(table) for table in tables()]
    bases, width = values.shape
    hbm = pl.BlockSpec(memory_space=pltpu.HBM)
    vmem = pl.BlockSpec(memory_space=pltpu.VMEM)

    def scratch(*shape):
        return pltpu.VMEM(shape, F32)

    operands = (values, gates, filters, skip.reshape(1, width), cotangent, flagged.reshape(2, SIDE))
    halfwords = jax.ShapeDtypeStruct((bases, width), BF16)
    home = (GROUPS // 2, 2, 8, SIDE)
    owner = (GROUPS, 8, SIDE)
    outs = pl.pallas_call(
        kernel,
        out_shape=[
            halfwords,
            halfwords,
            halfwords,
            jax.ShapeDtypeStruct(home, F32),
            jax.ShapeDtypeStruct((4, SIDE), F32),
        ],
        in_specs=[hbm] * 12,
        out_specs=[vmem] * 5,
        scratch_shapes=[
            *[pltpu.VMEM(array.shape, array.dtype) for array in (*operands, *constants)],
            scratch(GROUPS // 2, 2, 2, 8, SIDE),
            scratch(*home),
            scratch(GROUPS, 2, 8, SIDE),
            *[scratch(*owner)] * 4,
            *[scratch(*home)] * 2,
            scratch(bases, width),
            scratch(4, SIDE, 2 * SIDE),
            *[scratch(4, 2, SIDE, 2 * SIDE)] * 2,
            scratch(3, 4, 4, SIDE),
            pltpu.SemaphoreType.DMA((6,)),
            pltpu.SemaphoreType.DMA((6,)),
            pltpu.SemaphoreType.DMA((3,)),
            pltpu.SemaphoreType.DMA((3,)),
            pltpu.SemaphoreType.DMA((12,)),
        ],
        compiler_params=pltpu.CompilerParams(
            collective_id=0, has_side_effects=True, vmem_limit_bytes=28 << 20
        ),
        name="hyena",
    )(*[pltpu.with_memory_space_constraint(array, pltpu.HBM) for array in (*operands, *constants)])
    outs = pl.pallas_call(
        finish,
        out_shape=[
            halfwords,
            halfwords,
            halfwords,
            jax.ShapeDtypeStruct((bases, width), F32),
            jax.ShapeDtypeStruct((4, SIDE), F32),
        ],
        in_specs=[vmem] * 5,
        out_specs=[hbm] * 5,
        scratch_shapes=[scratch(bases, width), pltpu.SemaphoreType.DMA((5,))],
        compiler_params=pltpu.CompilerParams(vmem_limit_bytes=28 << 20),
        name="finish",
    )(*outs)
    return (*outs[:4], outs[4].reshape(width))


def solution(mesh):
    placed = (P("seq", "ch"), P("seq", "ch"), P("seq", "ch"), P("ch"), P("seq", "ch"), P("seq"))
    return jax.shard_map(
        body,
        mesh=mesh,
        in_specs=placed,
        out_specs=(P("seq", "ch"), P("seq", "ch"), P("seq", "ch"), P("seq", "ch"), P("ch")),
        check_vma=False,
    )
```

```python
import functools
import math

import jax
import jax.numpy as jnp
import ml_dtypes
import numpy as np
from jax import lax
from jax.experimental import pallas as pl
from jax.experimental.pallas import tpu as pltpu
from jax.sharding import PartitionSpec as P

MESH = pl.DeviceIdType.MESH
F32 = jnp.float32
BF16 = jnp.bfloat16
SEQ = 64
SIDE = 128
GROUPS = 128


def halves(table):
    high = table.astype(ml_dtypes.bfloat16)
    low = (table - high.astype(np.float64)).astype(ml_dtypes.bfloat16)
    return high, low


def tables():
    freq = np.arange(SIDE)
    coarse = np.arange(SIDE)
    order = np.concatenate([2 * np.arange(SEQ), 2 * np.arange(SEQ) + 1])
    angle = 2 * math.pi * ((2 * freq[:, None] + 1) * order[None, :] % 512) / 512
    first = np.concatenate([np.cos(angle), -np.sin(angle)], axis=0)
    first_hi, first_lo = halves(first)
    first_in = np.concatenate([first_hi, first_hi, first_lo], axis=1)
    last_hi, last_lo = halves(first.T * 2.0**-14)
    last_out = np.concatenate([last_hi, last_hi, last_lo], axis=1)
    turn = 2 * math.pi * ((2 * freq[:, None] + 1) * coarse[None, :]) / 65536
    angle = 2 * math.pi * (coarse[:, None] * coarse[None, :] % SIDE) / SIDE
    cosine, sine = np.cos(angle), np.sin(angle)
    second = np.block([[cosine, -sine], [sine, cosine]])
    second_in = np.concatenate([halves(second)[0]] * 2 + [halves(second)[1]], axis=0)
    second_out = np.concatenate([halves(second.T)[0]] * 2 + [halves(second.T)[1]], axis=0)
    return (
        first_in,
        last_out,
        np.cos(turn).astype(np.float32),
        np.sin(turn).astype(np.float32),
        second_in,
        second_out,
    )


def split(array):
    high = array.astype(BF16)
    return high, (array - high.astype(F32)).astype(BF16)


def dot(left, right):
    return jnp.dot(left, right, preferred_element_type=F32)


def second_step(parts, table):
    high, low = split(jnp.concatenate(parts, axis=0))
    return dot(jnp.concatenate([high, low, high], axis=1), table)


def rotate(both, cosine, sine):
    turned = []
    for side in range(2):
        real = both[:SIDE, side * SIDE : (side + 1) * SIDE]
        imag = both[SIDE:, side * SIDE : (side + 1) * SIDE]
        turned.append(
            jnp.concatenate([real * cosine + imag * sine, imag * cosine - real * sine], axis=1)
        )
    return turned


def rotate_back(both, cosine, sine):
    real, imag = both[:, :SIDE], both[:, SIDE:]
    return real * cosine - imag * sine, imag * cosine + real * sine


def times(left, right):
    lr, li, rr, ri = left[:, :SIDE], left[:, SIDE:], right[:, :SIDE], right[:, SIDE:]
    return jnp.concatenate([lr * rr - li * ri, lr * ri + li * rr], axis=1)


def conj_times(left, right):
    lr, li, rr, ri = left[:, :SIDE], left[:, SIDE:], right[:, :SIDE], right[:, SIDE:]
    return jnp.concatenate([lr * rr + li * ri, lr * ri - li * rr], axis=1)


def add_conj(left, right):
    return jnp.concatenate(
        [left[:, :SIDE] + right[:, :SIDE], left[:, SIDE:] - right[:, SIDE:]], axis=1
    )


def conj(array):
    return jnp.concatenate([array[:, :SIDE], -array[:, SIDE:]], axis=1)


def kernel(
    values_hbm, gates_hbm, filters_hbm, skip_hbm, cotangent_hbm, flagged_hbm,
    first_in_hbm, last_out_hbm, cosine_hbm, sine_hbm, second_in_hbm, second_out_hbm,
    mixed, value_grad, gate_grad, ret_fg, skip_grad,
    values, gates, filters, skip, cotangent, flagged,
    first_in, last_out, cosine, sine, second_in, second_out,
    send_fv, send_w, recv_fv, recv_w,
    back_mix, back_vg, back_fg, ret_mix, ret_vg,
    inner, kept_k, kept_v, kept_w, sums,
    send_sem, recv_sem, sums_send, sums_recv, fetch_sem, ready,
):
    fetches = [
        pltpu.make_async_copy(src, dst, fetch_sem.at[i])
        for i, (src, dst) in enumerate(
            (
                (filters_hbm, filters),
                (values_hbm, values),
                (gates_hbm, gates),
                (cotangent_hbm, cotangent),
                (flagged_hbm, flagged),
                (skip_hbm, skip),
                (first_in_hbm, first_in),
                (last_out_hbm, last_out),
                (cosine_hbm, cosine),
                (sine_hbm, sine),
                (second_in_hbm, second_in),
                (second_out_hbm, second_out),
            )
        )
    ]
    fetches[0].start()

    seq = lax.axis_index("seq")
    ch = lax.axis_index("ch")
    outer = (ch == 0) | (ch == 3)
    mirror = ch // 2

    peer_ch = [jnp.where(outer, 1, 0), jnp.where(outer, 2, 3)]
    group_sign = 1 - 2 * mirror
    group_base = 127 * mirror
    mine = seq + SEQ * mirror

    x, y, rest = seq // 16, seq // 4 % 4, seq % 4
    along_x = [(x + step) % 4 * 16 for step in range(4)]
    along_y = [(y + step) % 4 * 4 for step in range(4)]

    along_rest = [(rest + step) % 4 for step in range(4)]

    def column(there, visit):
        for k in range(8):
            visit(there + along_rest[k % 4], k // 4, peer_ch[k // 4])

    def peers(visit, near=True):
        def some(step, carry):
            far_x = (x + jnp.where(step == 0, 2, 2 * step - 1)) % 4 * 16
            for far_y in (2, 1, 3, 0):
                column(far_x + along_y[far_y], visit)
            return carry

        lax.fori_loop(0, 3, some, 0)
        for far_y in (2, 1, 3):
            column(x * 16 + along_y[far_y], visit)
        if near:
            column(seq - rest, visit)

    barrier = pltpu.get_barrier_semaphore()

    def greet(there, half, ch_there):
        pl.semaphore_signal(barrier, inc=1, device_id=(there, ch_there), device_id_type=MESH)

    circles = [
        (x, [along_x[k] + seq % 16 for k in range(1, 4)]),
        (y, [x * 16 + along_y[k] + rest for k in range(1, 4)]),
        (rest, [seq - rest + (rest + k) % 4 for k in range(1, 4)]),
    ]

    column(seq - rest, greet)
    plane = [px + py + rest for px in along_x for py in along_y][1:]
    for there in (*circles[2][1], *plane):
        pl.semaphore_signal(barrier, inc=1, device_id=(there, ch), device_id_type=MESH)
    for fetch in fetches[1:]:
        fetch.start()

    def remote(src, dst, which, there, ch_there):
        pltpu.make_async_remote_copy(
            src_ref=src,
            dst_ref=dst,
            send_sem=send_sem.at[which],
            recv_sem=recv_sem.at[which],
            device_id=(there, ch_there),
            device_id_type=MESH,
        ).start()

    def to_owner(src, dst, which):
        def visit(there, half, ch_there):
            group = group_base + group_sign * (half * SEQ + there)
            remote(src.at[group // 2, group % 2], dst.at[mirror * SEQ + seq], which, there, ch_there)

        return visit

    def to_home(src, dst, which):
        def visit(there, half, ch_there):
            group = mine + half * (127 - 2 * mine)
            remote(src.at[half * SEQ + there], dst.at[group // 2, group % 2], which, there, ch_there)

        peers(visit)

    def wait_for(semaphores, which, ref):
        pltpu.make_async_copy(ref, ref, semaphores.at[which]).wait()

    def send_sums(stage, total):
        place, others = circles[stage]
        sums[stage, place] = total
        for there in others:
            pltpu.make_async_remote_copy(
                src_ref=sums.at[stage, place],
                dst_ref=sums.at[stage, place],
                send_sem=sums_send.at[stage],
                recv_sem=sums_recv.at[stage],
                device_id=(there, ch),
                device_id_type=MESH,
            ).start()

    def summed(stage):
        wait_for(sums_recv, stage, sums.at[stage, pl.ds(0, 3)])
        wait_for(sums_send, stage, sums.at[stage, pl.ds(0, 3)])
        return (sums[stage, 0] + sums[stage, 1]) + (sums[stage, 2] + sums[stage, 3])

    rows = lax.broadcasted_iota(jnp.int32, (16, 8, SIDE), 1) < 4

    def block(half, part):
        return pl.ds(half * SIDE, SIDE), pl.ds(part * SIDE, SIDE)

    def pack(top, bottom):
        top, bottom = top.reshape(16, 8, SIDE), bottom.reshape(16, 8, SIDE)
        even = jnp.where(rows, top, pltpu.roll(bottom, 4, 1))
        odd = jnp.where(rows, pltpu.roll(top, 4, 1), bottom)
        return even, odd

    def unpack(even, odd):
        top = jnp.where(rows, even, pltpu.roll(odd, 4, 1))
        bottom = jnp.where(rows, pltpu.roll(even, 4, 1), odd)
        return top.reshape(SIDE, SIDE), bottom.reshape(SIDE, SIDE)

    def pack_all(source, dst, which):
        for part in range(4):
            here = pl.ds(part * 16, 16)
            turned = [source[block(half, part)].astype(F32).T for half in range(2)]
            dst[here, 0, which], dst[here, 1, which] = pack(*turned)

    fetches[0].wait()
    pack_all(filters, send_fv, 0)
    fetches[1].wait()
    pack_all(values, send_fv, 1)
    pl.semaphore_wait(barrier, 26)
    for there in plane:
        pl.semaphore_signal(ready, inc=1, device_id=(there, ch), device_id_type=MESH)
    column(seq - rest, to_owner(send_fv, recv_fv, 0))
    pl.semaphore_wait(ready, 15)
    peers(to_owner(send_fv, recv_fv, 0), near=False)

    for fetch in fetches[2:]:
        fetch.wait()
    flags = [
        jnp.broadcast_to(flagged[half : half + 1, :].astype(F32), (SIDE, SIDE)).T
        for half in range(2)
    ]
    totals = []
    for part in range(4):
        here = pl.ds(part * 16, 16)
        turned = []
        total = jnp.zeros((1, SIDE), F32)
        for half in range(2):
            at = block(half, part)
            product = gates[at].astype(F32) * (cotangent[at].astype(F32) * flags[half])
            inner[at] = product
            turned.append(product.T)
            total += jnp.sum(values[at].astype(F32) * product, axis=0, keepdims=True)
        send_w[here, 0], send_w[here, 1] = pack(*turned)
        totals.append(total)
    send_sums(0, jnp.concatenate(totals, axis=0))
    peers(to_owner(send_w, recv_w, 2))

    cos_turn, sin_turn = cosine[...], sine[...]

    def load_pair(ref, pair, which=0, count=1):
        flat = ref.reshape(2 * SEQ * count * 8, SIDE)
        stride = count * 8
        first = [
            flat[pl.ds(which * 8 + 4 * half + pair, SEQ, stride=stride), :] for half in range(2)
        ]
        start = SEQ * stride + which * 8 + 3 - pair
        second = [flat[pl.ds(start + 4 * half, SEQ, stride=stride), :] for half in range(2)]
        return jnp.concatenate(
            [jnp.concatenate(first, axis=0), jnp.concatenate(second, axis=0)], axis=1
        )

    def store_pair(ref, pair, result):
        flat = ref.reshape(2 * SEQ * 8, SIDE)
        for half in range(2):
            top = result[half * SEQ : (half + 1) * SEQ]
            flat[pl.ds(4 * half + pair, SEQ, stride=8), :] = top[:, :SIDE]
            flat[pl.ds(SEQ * 8 + 4 * half + 3 - pair, SEQ, stride=8), :] = top[:, SIDE:]

    def first_step(signal):
        high, low = split(signal)
        return dot(first_in[...], jnp.concatenate([high, low, high], axis=0))

    def first_step_exact(signal):
        high = signal.astype(BF16)
        return dot(first_in[:, SIDE:], jnp.concatenate([high, high], axis=0))

    def spectra(stepped):
        both = second_step(rotate(stepped, cos_turn, sin_turn), second_in[...])
        return both[:SIDE], both[SIDE:]

    def inverse(first, second):
        both = second_step([first, second], second_out[...])
        r0, i0 = rotate_back(both[:SIDE], cos_turn, sin_turn)
        r1, i1 = rotate_back(both[SIDE:], cos_turn, sin_turn)
        stacked = jnp.concatenate(
            [jnp.concatenate([r0, r1], axis=1), jnp.concatenate([i0, i1], axis=1)], axis=0
        )
        high, low = split(stacked)
        return dot(last_out[...], jnp.concatenate([high, low, high], axis=0))

    wait_for(recv_sem, 0, recv_fv)
    for pair in range(4):
        kept_k[pair] = add_conj(*spectra(first_step(load_pair(recv_fv, pair, 0, 2))))
    for pair in range(4):
        v0, v1 = spectra(first_step_exact(load_pair(recv_fv, pair, 1, 2)))
        kept_v[pair, 0], kept_v[pair, 1] = v0, v1
        k = kept_k[pair]
        store_pair(back_mix, pair, inverse(times(k, v0), conj_times(k, v1)))
    to_home(back_mix, ret_mix, 3)
    send_sums(1, summed(0))

    wait_for(recv_sem, 2, recv_w)
    for pair in range(4):
        w0, w1 = spectra(first_step(load_pair(recv_w, pair)))
        kept_w[pair, 0], kept_w[pair, 1] = w0, w1
        k = kept_k[pair]
        store_pair(back_vg, pair, inverse(conj_times(k, w0), times(k, w1)))
    to_home(back_vg, ret_vg, 4)
    send_sums(2, summed(1))
    for pair in range(4):
        product = add_conj(
            conj_times(kept_v[pair, 0], kept_w[pair, 0]),
            conj_times(kept_v[pair, 1], kept_w[pair, 1]),
        )
        store_pair(back_fg, pair, inverse(product, conj(product)))
    to_home(back_fg, ret_fg, 5)

    def returned(ref, part):
        here = pl.ds(part * 16, 16)
        top, bottom = unpack(ref[here, 0], ref[here, 1])
        return top.T, bottom.T

    wait_for(recv_sem, 3, ret_mix)
    for part in range(4):
        for half, result in enumerate(returned(ret_mix, part)):
            at = block(half, part)
            result = result + skip[:, at[1]] * values[at].astype(F32)
            mixed[at] = (gates[at].astype(F32) * result).astype(BF16)
            gate_grad[at] = (cotangent[at].astype(F32) * flags[half] * result).astype(BF16)
    skip_grad[...] = summed(2) * 2.0**-7
    wait_for(recv_sem, 4, ret_vg)
    for part in range(4):
        for half, result in enumerate(returned(ret_vg, part)):
            at = block(half, part)
            value_grad[at] = (result + skip[:, at[1]] * inner[at]).astype(BF16)
    for which, ref in ((0, recv_fv), (2, recv_w), (3, ret_mix), (4, ret_vg), (5, ret_fg)):
        wait_for(send_sem, which, ref)
    wait_for(recv_sem, 5, ret_fg)


def finish(*refs):
    arrived, outs, (turned, out_sem) = refs[:5], refs[5:10], refs[10:]
    stores = [
        pltpu.make_async_copy(src, dst, out_sem.at[i])
        for i, (src, dst) in enumerate(zip((*arrived[:3], turned, arrived[4]), outs))
    ]
    for i in (0, 1, 2, 4):
        stores[i].start()
    ret_fg = arrived[3]
    rows = lax.broadcasted_iota(jnp.int32, (16, 8, SIDE), 1) < 4
    for part in range(4):
        even, odd = ret_fg[pl.ds(part * 16, 16), 0], ret_fg[pl.ds(part * 16, 16), 1]
        top = jnp.where(rows, even, pltpu.roll(odd, 4, 1)).reshape(SIDE, SIDE)
        bottom = jnp.where(rows, pltpu.roll(even, 4, 1), odd).reshape(SIDE, SIDE)
        for half, result in enumerate((top, bottom)):
            turned[pl.ds(half * SIDE, SIDE), pl.ds(part * SIDE, SIDE)] = result.T * 2.0**-7
    stores[3].start()
    for store in stores:
        store.wait()


def body(values, gates, filters, skip, cotangent, flagged):
    constants = [jnp.asarray(table) for table in tables()]
    bases, width = values.shape
    hbm = pl.BlockSpec(memory_space=pltpu.HBM)
    vmem = pl.BlockSpec(memory_space=pltpu.VMEM)

    def scratch(*shape):
        return pltpu.VMEM(shape, F32)

    operands = (values, gates, filters, skip.reshape(1, width), cotangent, flagged.reshape(2, SIDE))
    halfwords = jax.ShapeDtypeStruct((bases, width), BF16)
    home = (GROUPS // 2, 2, 8, SIDE)
    owner = (GROUPS, 8, SIDE)
    outs = pl.pallas_call(
        kernel,
        out_shape=[
            halfwords,
            halfwords,
            halfwords,
            jax.ShapeDtypeStruct(home, F32),
            jax.ShapeDtypeStruct((4, SIDE), F32),
        ],
        in_specs=[hbm] * 12,
        out_specs=[vmem] * 5,
        scratch_shapes=[
            *[pltpu.VMEM(array.shape, array.dtype) for array in (*operands, *constants)],
            scratch(GROUPS // 2, 2, 2, 8, SIDE),
            scratch(*home),
            scratch(GROUPS, 2, 8, SIDE),
            *[scratch(*owner)] * 4,
            *[scratch(*home)] * 2,
            scratch(bases, width),
            scratch(4, SIDE, 2 * SIDE),
            *[scratch(4, 2, SIDE, 2 * SIDE)] * 2,
            scratch(3, 4, 4, SIDE),
            pltpu.SemaphoreType.DMA((6,)),
            pltpu.SemaphoreType.DMA((6,)),
            pltpu.SemaphoreType.DMA((3,)),
            pltpu.SemaphoreType.DMA((3,)),
            pltpu.SemaphoreType.DMA((12,)),
            pltpu.SemaphoreType.REGULAR,
        ],
        compiler_params=pltpu.CompilerParams(
            collective_id=0, has_side_effects=True, vmem_limit_bytes=28 << 20
        ),
        name="hyena",
    )(*[pltpu.with_memory_space_constraint(array, pltpu.HBM) for array in (*operands, *constants)])
    outs = pl.pallas_call(
        finish,
        out_shape=[
            halfwords,
            halfwords,
            halfwords,
            jax.ShapeDtypeStruct((bases, width), F32),
            jax.ShapeDtypeStruct((4, SIDE), F32),
        ],
        in_specs=[vmem] * 5,
        out_specs=[hbm] * 5,
        scratch_shapes=[scratch(bases, width), pltpu.SemaphoreType.DMA((5,))],
        compiler_params=pltpu.CompilerParams(vmem_limit_bytes=28 << 20),
        name="finish",
    )(*outs)
    return (*outs[:4], outs[4].reshape(width))


def solution(mesh):
    placed = (P("seq", "ch"), P("seq", "ch"), P("seq", "ch"), P("ch"), P("seq", "ch"), P("seq"))
    return jax.shard_map(
        body,
        mesh=mesh,
        in_specs=placed,
        out_specs=(P("seq", "ch"), P("seq", "ch"), P("seq", "ch"), P("seq", "ch"), P("ch")),
        check_vma=False,
    )
```
